32 devices in a mesh: cells: 8 (over z, x), cols: 4 (over y, core).
Axes of the slice: x: 2, y: 2, z: 4, core: 2. Of those that a mesh axis runs over, the one named last changes fastest.
Arguments:
- current: float32 [64, 256, 256], P('cells', 'cols'), may hold values from -6 to 6
- voltage: float32 [64, 256, 256], P('cells', 'cols'), may hold values from -6 to 6
- resistance: float32 [64, 256], P('cells'), may hold values from 0.1 to 1
- elastance: float32 [64, 256], P('cells'), may hold values from 0.1 to 1
- port_gain: float32 [64, 256], P('cells'), may hold values from -6 to 6
- symbols: int32 [3, 32, 256], P(None, 'cells'), may hold values from 0 to 3
- neighbours: int32 [64, 16], P('cells'), may hold values from 0 to 63, as said below
- live_counts: int32 [64], P('cells'), may hold values from 1 to 16, as said below
- membership: int32 [64, 1], P('cells'), may hold values from 0 to 15
- inductance_near: bfloat16 [64, 16, 256, 256], P('cells', None, 'cols'), may hold values from -0.09375 to 0.09375
- source_basis: bfloat16 [64, 64, 256], P('cells'), may hold values from -0.1875 to 0.1875
- target_basis: bfloat16 [64, 64, 256], P('cells'), may hold values from -0.75 to 0.75
- translation: bfloat16 [1024, 1024], replicated, may hold values from -0.1875 to 0.1875
Outputs:
- final_current: float32 [64, 256, 256], P('cells', 'cols')
- final_voltage: float32 [64, 256, 256], P('cells', 'cols')
The draws below stay inside these ranges and needn't reach their ends.
Inputs may be any that keep to these rules, and one draw needn't show every extreme that they name: `neighbours`: entry 0 of block row t is t itself; every entry names a block at most 8 blocks from t. Block row t uses the first live_counts[t] entries of its list. `membership`: every cluster has at least one block.
All inputs are finite; a program needn't handle non-finite values.
Results may differ from the reference program's by a relative error of at most 0.003.
Values may be sent and summed in bfloat16 or wider, within the bound.
No kernel may reach another device: no remote copies, remote signals or barrier semaphores. Data moves between devices by JAX's collectives and lax.ppermute only.
A program may use at most 64 MiB of HBM per device.

```python
import math
import jax
import jax.numpy as jnp
from jax import lax

CB = 256
RANK = 64
NEAR = 16
REACH = 8
CLUSTERS = 16
STEPS = 3
SCENARIOS = 256
BLOCKS = 64
LANES = 32


def draw_neighbours(key, part):
    row_keys = jax.random.split(key, BLOCKS)
    offsets_all = jnp.concatenate([-jnp.arange(1, REACH + 1, dtype=jnp.int32), jnp.arange(1, REACH + 1, dtype=jnp.int32)])

    def pick_offsets(row_key):
        return jax.random.permutation(row_key, offsets_all)[:NEAR - 1]
    offsets = jax.vmap(pick_offsets)(row_keys)
    offsets = jnp.concatenate([jnp.zeros((BLOCKS, 1), jnp.int32), offsets], axis=1)
    row_ids = jnp.arange(BLOCKS, dtype=jnp.int32)[:, None]
    targets = row_ids + offsets
    outside = (targets < 0) | (targets >= BLOCKS)
    return jnp.where(outside, row_ids - offsets, targets).astype(jnp.int32)


def draw_live_counts(key, part):
    split_keys = jax.random.split(key, 3)
    counts_drawn = jax.random.randint(split_keys[0], (BLOCKS,), 1, NEAR + 1)
    full_row = jax.random.randint(split_keys[1], (), 0, BLOCKS)
    short_row = (full_row + 1 + jax.random.randint(split_keys[2], (), 0, BLOCKS - 1)) % BLOCKS
    return counts_drawn.at[full_row].set(NEAR).at[short_row].set(1).astype(jnp.int32)


def set_ends(entries, rng, low, high):
    longest = entries.shape.index(max(entries.shape))
    spots = []
    for shift in (0, 1):
        where = [jax.random.randint(jax.random.fold_in(rng, axis), (), 0, length) for axis, length in enumerate(entries.shape)]
        where[longest] = (where[longest] + shift) % entries.shape[longest]
        spots.append(tuple(where))
    return entries.at[spots[0]].set(low).at[spots[1]].set(high)


def level_of(rng, dims, cuts, low, largest):
    factor_of, own = 1.0, jax.random.fold_in(rng, 6)
    for position, parts in cuts:
        heights = jnp.exp(jax.random.uniform(jax.random.fold_in(own, position), (parts,), jnp.float32, low / len(cuts), largest / len(cuts)))
        factor_of = factor_of * jnp.repeat(heights, dims[position] // parts).reshape([-1 if axis == position else 1 for axis in range(len(dims))])
    return factor_of


def different_ones(own_key, rows, number_of, top, lift):
    ranking = jax.random.permutation(jax.random.fold_in(own_key, 1), number_of)
    boost = ranking
    for power in range(3):
        boost = boost * boost // number_of
    boost = boost * lift // number_of
    tickets = jax.random.randint(jax.random.fold_in(own_key, 2), (rows, number_of), 0, 4096) + boost
    holders = jax.random.permutation(jax.random.fold_in(own_key, 3), rows)[jnp.arange(number_of) % rows]
    tickets = jnp.where(jnp.arange(rows)[:, None] == holders[None, :], 1 << 14, tickets)
    priority = tickets * number_of + jnp.arange(number_of)
    return lax.top_k(priority.astype(jnp.int32), top)[1].astype(jnp.int32)


def scatter_about(own_key, dims, width, reach, cuts=(), kind=jnp.bfloat16):
    array = jax.random.normal(own_key, dims, jnp.float32) * width
    if len(cuts) > 0:
        array = level_of(own_key, dims, cuts, -0.22, 0.18) * array
    return jnp.clip(array, min=-reach, max=reach).astype(kind)


def setup_inputs(seed: int = 0) -> dict:
    key_list = jax.random.split(jax.random.key(seed), 14)
    current = scatter_about(key_list[0], (BLOCKS, CB, SCENARIOS), 1.0, 6.0, ((0, 8), (1, 4)), jnp.float32)
    voltage = scatter_about(key_list[1], (BLOCKS, CB, SCENARIOS), 1.0, 6.0, ((0, 8), (1, 4)), jnp.float32)
    resistance = jnp.clip(jnp.exp(math.log(1.0) - 2.3025851 * jax.random.uniform(key_list[2], (BLOCKS, CB), jnp.float32) ** level_of(key_list[2], (BLOCKS, CB), ((0, 8),), -0.2, 0.2)), 0.1, 1.0)
    elastance = jnp.clip(jnp.exp(math.log(1.0) - 2.3025851 * jax.random.uniform(key_list[3], (BLOCKS, CB), jnp.float32) ** level_of(key_list[3], (BLOCKS, CB), ((0, 8),), -0.2, 0.2)), 0.1, 1.0)
    port_gain = scatter_about(key_list[4], (BLOCKS, CB), 1.0, 6.0, ((0, 8),), jnp.float32)
    symbols = set_ends(jax.random.randint(key_list[5], (STEPS, LANES, SCENARIOS), 0, 4), jax.random.fold_in(key_list[5], 1), 0, 3).astype(jnp.int32)
    neighbours = draw_neighbours(jax.random.fold_in(key_list[13], 71), 0)
    live_counts = draw_live_counts(jax.random.fold_in(key_list[13], 71), 0)
    membership = different_ones(key_list[8], BLOCKS, CLUSTERS, 1, 512)
    inductance_near = scatter_about(key_list[9], (BLOCKS, NEAR, CB, CB), (NEAR * CB) ** -0.5, 0.09375, ((0, 8), (2, 4)))
    source_basis = scatter_about(key_list[10], (BLOCKS, RANK, CB), (CB * BLOCKS // CLUSTERS) ** -0.5, 0.1875, ((0, 8),))
    target_basis = scatter_about(key_list[11], (BLOCKS, RANK, CB), RANK ** -0.5, 0.75, ((0, 8),))
    translation = scatter_about(key_list[12], (CLUSTERS * RANK, CLUSTERS * RANK), (CLUSTERS * RANK) ** -0.5, 0.1875)
    return dict(current=current, voltage=voltage, resistance=resistance, elastance=elastance, port_gain=port_gain, symbols=symbols, neighbours=neighbours, live_counts=live_counts, membership=membership, inductance_near=inductance_near, source_basis=source_basis, target_basis=target_basis, translation=translation)


def reference(current, voltage, resistance, elastance, port_gain, symbols, neighbours, live_counts, membership, inductance_near, source_basis, target_basis, translation):
    levels = (2 * symbols - 3).astype(jnp.float32) / 3.0
    member = membership[:, 0]
    entry_index = jnp.arange(NEAR, dtype=jnp.int32)
    translation_wide = translation.astype(jnp.float32)
    for marching in range(STEPS):
        lane_level = jnp.repeat(levels[marching], 2, axis=0)
        drive_volts = port_gain[:, :, None] * lane_level[:, None, :]
        excitation = (drive_volts - resistance[:, :, None] * current - voltage).astype(jnp.bfloat16)

        def near_row(packed):
            index_row, live_count, block_matrix = packed
            selected_blocks = excitation[index_row]
            selected_blocks = jnp.where((entry_index < live_count)[:, None, None], selected_blocks, jnp.zeros((), jnp.bfloat16))
            return jnp.dot(block_matrix.reshape(NEAR * CB, CB).T, selected_blocks.reshape(NEAR * CB, SCENARIOS), preferred_element_type=jnp.float32)

        near_field = lax.map(near_row, (neighbours, live_counts, inductance_near))
        coefficients = jnp.einsum("bkc,bcs->bks", source_basis.astype(jnp.float32), excitation.astype(jnp.float32), precision=lax.Precision.HIGHEST)
        totals = jax.ops.segment_sum(coefficients, member, num_segments=CLUSTERS)
        translated = jnp.dot(translation_wide, totals.reshape(CLUSTERS * RANK, SCENARIOS), precision=lax.Precision.HIGHEST)
        translated = translated.reshape(CLUSTERS, RANK, SCENARIOS)
        chosen = translated[member]
        far_field = jnp.einsum("bkr,bks->brs", target_basis.astype(jnp.float32), chosen, precision=lax.Precision.HIGHEST)
        current = current + near_field + far_field
        voltage = voltage + elastance[:, :, None] * current
    return (current, voltage)
```

```python
import functools

import jax
import jax.numpy as jnp
from jax import lax
from jax.experimental import pallas as pl
from jax.experimental.pallas import tpu as pltpu
from jax.sharding import PartitionSpec as P

CLUSTERS = 16
STEPS = 3
BF = jnp.bfloat16
F32 = jnp.float32
I16 = jnp.int16
TILE = 16
SMEM = pl.BlockSpec(memory_space=pltpu.SMEM)
VMEM = pl.BlockSpec(memory_space=pltpu.VMEM)
HBM = pl.BlockSpec(memory_space=pltpu.HBM)
ANY = pl.BlockSpec(memory_space=pl.ANY)


def local_call(body, ins, outs, scratch=(), scalars=0, after=(), where=VMEM, flops=0):
    specs = [SMEM] * scalars + [where] * (len(ins) - scalars) + [ANY] * len(after)
    moved = sum(a.size * a.dtype.itemsize for a in ins) + sum(o.size * o.dtype.itemsize for o in outs)

    def run(*refs):
        body(*refs[: len(ins)], *refs[len(ins) + len(after) :])

    return pl.pallas_call(
        run,
        out_shape=tuple(outs),
        in_specs=specs,
        out_specs=tuple(VMEM for _ in outs),
        scratch_shapes=list(scratch),
        compiler_params=pltpu.CompilerParams(vmem_limit_bytes=16 << 20),
        cost_estimate=pl.CostEstimate(flops=flops, bytes_accessed=moved, transcendentals=0),
    )(*ins, *after)


def shaped(shape, dtype):
    return jax.ShapeDtypeStruct(shape, dtype)


def pick(flag, one, zero):
    return jnp.where(flag == 1, one, zero)


def top(x):
    return jnp.max(jnp.abs(x).reshape(x.shape[0] // 8, 8, x.shape[1]), axis=0)


def exponent(bound):
    return jnp.ceil(jnp.log2(jnp.maximum(bound, 1e-30)))


def scaled(x, factor):
    return (x.reshape(x.shape[0] // 8, 8, x.shape[1]) * factor[None]).reshape(x.shape)


def encode(x, power):
    return jnp.round(scaled(x, jnp.exp2(14.0 - power))).astype(jnp.int32).astype(I16)


def decode(x, power):
    return scaled(x.astype(jnp.int32).astype(F32), jnp.exp2(power - 14.0))


def put_powers(ref, first, second):
    ref[...] = jnp.concatenate([first, second], axis=0).astype(jnp.int32).astype(I16)


def get_powers(ref):
    both = ref[...].astype(jnp.int32).astype(F32)
    return both[:8], both[8:]


def split(x):
    high = x.astype(BF)
    return high, (x - high.astype(F32)).astype(BF)


def drive(step, b, blocks, symbols_ref, cells_ref):
    lane = b * symbols_ref.shape[1] // blocks
    level = (2 * symbols_ref[step, lane : lane + 1, :] - 3).astype(F32) / 3.0
    return cells_ref[0, :, b : b + 1] * level


def send_totals(wide_ref, message):
    clusters, ranks, _ = wide_ref.shape
    power = exponent(functools.reduce(jnp.maximum, [top(wide_ref[g]) for g in range(clusters)]))
    for g in range(clusters):
        message[g * ranks : (g + 1) * ranks, :] = encode(wide_ref[g], power)
    put_powers(message.at[clusters * ranks :, :], power, power)


def first_kernel(
    blocks, meta, current, voltage, port, resist, elast, symbols,
    excite_ref, other_ref, cells_ref, damp_ref, cur, vol, flat, syms, turned, sems,
):
    share = current.shape[1]
    core, col = meta[0], meta[2]
    copies = [
        pltpu.make_async_copy(source, target, sems.at[k])
        for k, (source, target) in enumerate(
            [
                (port, flat.at[0]),
                (resist, flat.at[1]),
                (elast, flat.at[2]),
                (symbols, syms),
                (current, cur),
                (voltage, vol),
            ]
        )
    ]
    for copy in copies:
        copy.start()
    for k in range(3):
        copies[k].wait()
        turned[k] = flat[k].T
        cells_ref[k] = turned[k, pl.ds(pl.multiple_of(col * share, share), share), :]
    damp_ref[...] = turned[1] + turned[2]
    for copy in copies[3:]:
        copy.wait()
    half = cur.shape[2] // 2
    for b in range(blocks):
        excite = (
            drive(0, b, blocks, syms, cells_ref) - cells_ref[1, :, b : b + 1] * cur[b] - vol[b]
        ).astype(BF)
        excite_ref[b] = excite
        other_ref[b] = pick(core, excite[:, :half], excite[:, half:])


def source_kernel(meta, excite, other, basis, message, keep_ref, ready):
    blocks, share, scen = excite.shape
    rank, half = basis.shape[1] // 2, scen // 2
    core, row = meta[0], meta[1]
    bound = jnp.zeros((8, half), F32)
    for b in range(blocks):
        own = pick(core, excite[b, :, half:], excite[b, :, :half])
        got = other[b]
        chip = jnp.concatenate([pick(core, got, own), pick(core, own, got)], axis=0)
        side = basis[b, :, pl.ds(pl.multiple_of(row * 2 * share, 2 * share), 2 * share)]
        part = jnp.dot(side, chip, preferred_element_type=F32)
        keep_ref[b] = pick(row, part[rank:], part[:rank])
        sent = pick(row, part[:rank], part[rank:])
        ready[b] = sent
        bound = jnp.maximum(bound, top(sent))
    power = exponent(bound)
    for b in range(blocks):
        message[b * rank : (b + 1) * rank, :] = encode(ready[b], power)
    put_powers(message.at[blocks * rank :, :], power, power)


def cluster_kernel(member, kept, got, wide_ref, message):
    blocks, ranks, _ = kept.shape
    power, _ = get_powers(got.at[blocks * ranks :, :])
    wide_ref[...] = jnp.zeros(wide_ref.shape, F32)
    for b in range(blocks):
        wide_ref[member[b]] += kept[b] + decode(got[b * ranks : (b + 1) * ranks, :], power)
    send_totals(wide_ref, message)


def add_kernel(wide, got, wide_ref, message):
    clusters, ranks, _ = wide.shape
    power, _ = get_powers(got.at[clusters * ranks :, :])
    for g in range(clusters):
        wide_ref[g] = wide[g] + decode(got[g * ranks : (g + 1) * ranks, :], power)
    send_totals(wide_ref, message)


def translate_kernel(meta, member, wide, got, translation, chosen_ref, totals, rows):
    clusters, ranks, scen = wide.shape
    row = meta[1]
    power, _ = get_powers(got.at[clusters * ranks :, :])
    for g in range(clusters):
        high, low = split(wide[g] + decode(got[g * ranks : (g + 1) * ranks, :], power))
        both = jnp.concatenate([high, low], axis=1)
        none = jnp.zeros(both.shape, BF)
        totals[2 * g * ranks : (2 * g + 1) * ranks, :] = pick(row, none, both)
        totals[(2 * g + 1) * ranks : (2 * g + 2) * ranks, :] = pick(row, both, none)
    blocks, rank = chosen_ref.shape[:2]
    for b in range(blocks):
        rows[b * rank : (b + 1) * rank, :] = translation[
            pl.ds(pl.multiple_of(member[b] * rank, rank), rank), :
        ]
    both = jnp.dot(rows[...], totals[...], preferred_element_type=F32)
    for b in range(blocks):
        block = both[b * rank : (b + 1) * rank]
        chosen_ref[b] = block[:, :scen] + block[:, scen:]


def near_kernel(places, induct, own, pair, past, part_ref, around, stacked):
    blocks, share = own.shape[:2]
    entries = places.shape[1]
    for k, source in enumerate((own, pair, past)):
        around[k * blocks : (k + 1) * blocks] = source[...]
    around[3 * blocks] = jnp.zeros(around.shape[1:], BF)
    for t in range(blocks):
        for j in range(entries):
            stacked[t % 2, j * share : (j + 1) * share, :] = around[places[t, j]]
        part_ref[t] = lax.dot_general(
            induct[t], stacked[t % 2], (((0,), (0,)), ((), ())), preferred_element_type=F32
        )


def finish_kernel(step, last, meta, part, chosen, target, *refs):
    blocks, cells, scen = part.shape
    half = scen // 2
    core, col = meta[0], meta[2]
    if last:
        message, keep_ref = refs
    else:
        current, voltage, cells_ref, damp, symbols, basis, message, keep_ref, coef_ref, change = refs
    share = keep_ref.shape[1] // 2
    for b in range(blocks):
        high, low = split(chosen[b])
        far = lax.dot_general(
            jnp.concatenate([target[b], target[b]], axis=0),
            jnp.concatenate([high, low], axis=0),
            (((0,), (0,)), ((), ())),
            preferred_element_type=F32,
        )
        none = jnp.zeros_like(far)
        total = part[b] + jnp.concatenate([pick(core, none, far), pick(core, far, none)], axis=1)
        quarters = [total[k * share : (k + 1) * share] for k in range(4)]
        keep_ref[b, :share, :] = pick(core, quarters[1], quarters[0])
        keep_ref[b, share:, :] = pick(core, quarters[3], quarters[2])
        sent = [pick(core, quarters[0], quarters[1]), pick(core, quarters[2], quarters[3])]
        power = exponent(jnp.maximum(top(sent[0]), top(sent[1])))
        for k in range(2):
            message[b, k * share : (k + 1) * share, :] = encode(sent[k], power)
        second = power
        if not last:
            change[...] = -damp[:, b : b + 1] * total
            rows = pl.ds(pl.multiple_of(col * share, share), share)
            change[rows, :] += (
                drive(step + 1, b, blocks, symbols, cells_ref)
                - voltage[b]
                - (cells_ref[1, :, b : b + 1] + cells_ref[2, :, b : b + 1]) * current[b]
            )
            high, low = split(change[...])
            coefs = jnp.dot(
                jnp.concatenate([basis[b], basis[b]], axis=1),
                jnp.concatenate([high, low], axis=0),
                preferred_element_type=F32,
            )
            own = pick(core, coefs[:, half:], coefs[:, :half])
            their = pick(core, coefs[:, :half], coefs[:, half:])
            rank = coefs.shape[0] // 2
            coef_ref[b] = jnp.concatenate([own[:rank], own[rank:]], axis=1)
            their = jnp.concatenate([their[:rank], their[rank:]], axis=1)
            second = exponent(top(their))
            message[b, 2 * share : 2 * share + rank, :] = encode(their, second)
        put_powers(message.at[b, message.shape[1] - TILE :, :], power, second)


def halve_kernel(last, meta, kept, got, *refs):
    blocks = kept.shape[0]
    row = meta[1]
    if last:
        message, keep_ref, ready = refs
    else:
        coefs, message, keep_ref, coef_ref, ready, ready_coefs = refs
    share = keep_ref.shape[1]
    scen = kept.shape[2]
    half = scen // 2
    bound = jnp.zeros((8, scen), F32)
    second = jnp.zeros((8, scen), F32)
    for b in range(blocks):
        power, power_coefs = get_powers(got.at[b, got.shape[1] - TILE :, :])
        low = kept[b, :share] + decode(got[b, :share], power)
        high = kept[b, share:] + decode(got[b, share : 2 * share], power)
        keep_ref[b] = pick(row, high, low)
        sent = pick(row, low, high)
        ready[b] = sent
        bound = jnp.maximum(bound, top(sent))
        if not last:
            rank = coefs.shape[1]
            both = coefs[b] + decode(got[b, 2 * share : 2 * share + rank], power_coefs)
            coef_ref[b] = pick(row, both[:, half:], both[:, :half])
            sent = pick(row, both[:, :half], both[:, half:])
            sent = jnp.concatenate([sent[: rank // 2], sent[rank // 2 :]], axis=1)
            ready_coefs[b] = sent
            second = jnp.maximum(second, top(sent))
    power = exponent(bound)
    for b in range(blocks):
        message[b * share : (b + 1) * share, :] = encode(ready[b], power)
    if not last:
        second = exponent(second)
        start, rows = blocks * share, ready_coefs.shape[1]
        for b in range(blocks):
            message[start + b * rows : start + (b + 1) * rows, :] = encode(ready_coefs[b], second)
    put_powers(message.at[message.shape[0] - TILE :, :], power, second if not last else power)


def update_kernel(step, last, *refs):
    if last:
        current, voltage, kept, got, cells, current_ref, voltage_ref = refs
    else:
        member, current, voltage, kept, got, cells, coefs, symbols = refs[:8]
        current_ref, voltage_ref, excite_ref, wide_ref, message = refs[8:]
    blocks, share, scen = current.shape
    power, second = get_powers(got.at[got.shape[0] - TILE :, :])
    for b in range(blocks):
        cur = current[b] + (kept[b] + decode(got[b * share : (b + 1) * share, :], power))
        vol = voltage[b] + cells[2, :, b : b + 1] * cur
        current_ref[b] = cur
        voltage_ref[b] = vol
        if not last:
            excite = drive(step + 1, b, blocks, symbols, cells) - cells[1, :, b : b + 1] * cur - vol
            excite_ref[b] = excite.astype(BF)
    if not last:
        wide_ref[...] = jnp.zeros(wide_ref.shape, F32)
        start, rows, half = blocks * share, coefs.shape[1] // 2, scen // 2
        for b in range(blocks):
            sent = decode(got[start + b * rows : start + (b + 1) * rows, :], second)
            sent = jnp.concatenate([sent[:, :half], sent[:, half:]], axis=0)
            wide_ref[member[b]] += coefs[b] + sent
        send_totals(wide_ref, message)


def swap(array, axis, distance):
    count = lax.axis_size(axis)
    return lax.ppermute(array, axis, [(i, i ^ distance) for i in range(count)])


def pass_on(array, axis):
    count = lax.axis_size(axis)
    up = [(i, i + 2) for i in range(0, count - 2, 2)]
    down = [(i, i - 2) for i in range(3, count, 2)]
    return lax.ppermute(array, axis, up + down)


def per_device(
    current,
    voltage,
    resistance,
    elastance,
    port_gain,
    symbols,
    neighbours,
    live_counts,
    membership,
    inductance_near,
    source_basis,
    target_basis,
    translation,
):
    blocks, entries = neighbours.shape
    share, cells = inductance_near.shape[2:]
    scen = current.shape[2]
    rank = source_basis.shape[1]
    groups = lax.axis_size("cells")
    half, hrank = scen // 2, rank // 2
    group, col = lax.axis_index("cells"), lax.axis_index("cols")
    meta = jnp.stack([col % 2, col // 2, col]).astype(jnp.int32)
    member = membership[:, 0]
    owner = neighbours // blocks
    slot = jnp.where(owner == group, 0, jnp.where(owner == (group ^ 1), 1, 2))
    live = jnp.arange(entries, dtype=jnp.int32)[None, :] < live_counts[:, None]
    places = jnp.where(live, slot * blocks + neighbours % blocks, 3 * blocks).astype(jnp.int32)
    induct = inductance_near.reshape(blocks, entries * share, cells)

    rows_f32 = shaped((blocks, share, scen), F32)
    rows_bf = shaped((blocks, share, scen), BF)
    wide_f32 = shaped((CLUSTERS, hrank, half), F32)
    wide_msg = shaped((CLUSTERS * hrank + TILE, half), I16)
    coef_f32 = shaped((blocks, hrank, half), F32)

    excite, other, columns, damp = local_call(
        functools.partial(first_kernel, blocks),
        (meta, current, voltage, port_gain, resistance, elastance, symbols),
        (
            rows_bf,
            shaped((blocks, share, half), BF),
            shaped((3, share, blocks), F32),
            shaped((cells, blocks), F32),
        ),
        scratch=(
            pltpu.VMEM(current.shape, F32),
            pltpu.VMEM(voltage.shape, F32),
            pltpu.VMEM((3,) + port_gain.shape, F32),
            pltpu.VMEM(symbols.shape, jnp.int32),
            pltpu.VMEM((3, cells, blocks), F32),
            pltpu.SemaphoreType.DMA((6,)),
        ),
        scalars=1,
        where=HBM,
    )
    for step in range(STEPS):
        last = step == STEPS - 1
        pair = swap(excite, "cells", 1)
        if step == 0:
            other = swap(other, "cols", 1)
            send, kept = local_call(
                source_kernel,
                (meta, excite, other, source_basis),
                (shaped((blocks * hrank + TILE, half), I16), coef_f32),
                scratch=(pltpu.VMEM((blocks, hrank, half), F32),),
                scalars=1,
            )
            got = swap(send, "cols", 2)
            wide, send = local_call(cluster_kernel, (member, kept, got), (wide_f32, wide_msg), scalars=1)
        distance = groups // 2
        while distance > 1:
            got = swap(send, "cells", groups // distance)
            wide, send = local_call(add_kernel, (wide, got), (wide_f32, wide_msg))
            distance //= 2
        got = swap(send, "cells", 1)
        (chosen,) = local_call(
            translate_kernel,
            (meta, member, wide, got, translation),
            (shaped((blocks, rank, half), F32),),
            scratch=(
                pltpu.VMEM((CLUSTERS * rank, scen), BF),
                pltpu.VMEM((blocks * rank, CLUSTERS * rank), BF),
            ),
            scalars=2,
        )
        past = pass_on(pair, "cells")
        (part,) = local_call(
            near_kernel,
            (places, induct, excite, pair, past),
            (shaped((blocks, cells, scen), F32),),
            scratch=(
                pltpu.VMEM((3 * blocks + 1, share, scen), BF),
                pltpu.VMEM((2, entries * share, scen), BF),
            ),
            scalars=1,
        )
        both_f32 = shaped((blocks, 2 * share, scen), F32)
        if last:
            send, kept = local_call(
                functools.partial(finish_kernel, step, last),
                (meta, part, chosen, target_basis),
                (shaped((blocks, 2 * share + TILE, scen), I16), both_f32),
                scalars=1,
            )
            got = swap(send, "cols", 1)
            send, kept = local_call(
                functools.partial(halve_kernel, last),
                (meta, kept, got),
                (shaped((blocks * share + TILE, scen), I16), rows_f32),
                scratch=(pltpu.VMEM((blocks, share, scen), F32),),
                scalars=1,
            )
            got = swap(send, "cols", 2)
            current, voltage = local_call(
                functools.partial(update_kernel, step, last),
                (current, voltage, kept, got, columns),
                (rows_f32, rows_f32),
            )
        else:
            send, kept, coefs = local_call(
                functools.partial(finish_kernel, step, last),
                (meta, part, chosen, target_basis, current, voltage, columns, damp, symbols, source_basis),
                (
                    shaped((blocks, 2 * share + hrank + TILE, scen), I16),
                    both_f32,
                    shaped((blocks, hrank, scen), F32),
                ),
                scratch=(pltpu.VMEM((cells, scen), F32),),
                scalars=1,
            )
            got = swap(send, "cols", 1)
            send, kept, coefs = local_call(
                functools.partial(halve_kernel, last),
                (meta, kept, got, coefs),
                (shaped((blocks * (share + hrank // 2) + TILE, scen), I16), rows_f32, coef_f32),
                scratch=(
                    pltpu.VMEM((blocks, share, scen), F32),
                    pltpu.VMEM((blocks, hrank // 2, scen), F32),
                ),
                scalars=1,
            )
            got = swap(send, "cols", 2)
            current, voltage, excite, wide, send = local_call(
                functools.partial(update_kernel, step, last),
                (member, current, voltage, kept, got, columns, coefs, symbols),
                (rows_f32, rows_f32, rows_bf, wide_f32, wide_msg),
                scalars=1,
            )
    return (current, voltage)


def solution(mesh):
    placed = (
        P("cells", "cols", None),
        P("cells", "cols", None),
        P("cells", None),
        P("cells", None),
        P("cells", None),
        P(None, "cells", None),
        P("cells", None),
        P("cells"),
        P("cells", None),
        P("cells", None, "cols", None),
        P("cells", None, None),
        P("cells", None, None),
        P(),
    )
    return jax.shard_map(
        per_device,
        mesh=mesh,
        in_specs=placed,
        out_specs=(P("cells", "cols", None), P("cells", "cols", None)),
        check_vma=False,
    )
```

```python
import functools

import jax
import jax.numpy as jnp
from jax import lax
from jax.experimental import pallas as pl
from jax.experimental.pallas import tpu as pltpu
from jax.sharding import PartitionSpec as P

CLUSTERS = 16
STEPS = 3
BF = jnp.bfloat16
F32 = jnp.float32
I16 = jnp.int16
TILE = 16
SMEM = pl.BlockSpec(memory_space=pltpu.SMEM)
VMEM = pl.BlockSpec(memory_space=pltpu.VMEM)
HBM = pl.BlockSpec(memory_space=pltpu.HBM)
ANY = pl.BlockSpec(memory_space=pl.ANY)


def local_call(body, ins, outs, scratch=(), scalars=0, after=(), left=()):
    moved = sum(a.size * a.dtype.itemsize for a in ins) + sum(o.size * o.dtype.itemsize for o in outs)
    specs = [SMEM] * scalars + [VMEM] * (len(ins) - scalars) + [ANY] * len(after)
    ins = list(ins)
    for k in left:
        specs[k] = HBM
        ins[k] = pltpu.with_memory_space_constraint(ins[k], pltpu.HBM)

    def run(*refs):
        body(*refs[: len(ins)], *refs[len(ins) + len(after) :])

    return pl.pallas_call(
        run,
        out_shape=tuple(outs),
        in_specs=specs,
        out_specs=tuple(VMEM for _ in outs),
        scratch_shapes=list(scratch),
        compiler_params=pltpu.CompilerParams(vmem_limit_bytes=16 << 20),
        cost_estimate=pl.CostEstimate(flops=0, bytes_accessed=moved, transcendentals=0),
        name=getattr(body, "func", body).__name__,
    )(*ins, *after)


def shaped(shape, dtype):
    return jax.ShapeDtypeStruct(shape, dtype)


def pick(flag, one, zero):
    return jnp.where(flag == 1, one, zero)


def top(x):
    return jnp.max(jnp.abs(x).reshape(x.shape[0] // 8, 8, x.shape[1]), axis=0)


def exponent(bound):
    return jnp.ceil(jnp.log2(jnp.maximum(bound, 1e-30)))


def scaled(x, factor):
    return (x.reshape(x.shape[0] // 8, 8, x.shape[1]) * factor[None]).reshape(x.shape)


def encode(x, power):
    return jnp.round(scaled(x, jnp.exp2(14.0 - power))).astype(jnp.int32).astype(I16)


def decode(x, power):
    return scaled(x.astype(jnp.int32).astype(F32), jnp.exp2(power - 14.0))


def put_powers(ref, first, second):
    ref[...] = jnp.concatenate([first, second], axis=0).astype(jnp.int32).astype(I16)


def get_powers(ref):
    both = ref[...].astype(jnp.int32).astype(F32)
    return both[:8], both[8:]


def split(x):
    high = x.astype(BF)
    return high, (x - high.astype(F32)).astype(BF)


def drive(step, b, blocks, symbols_ref, cells_ref):
    lane = b * symbols_ref.shape[1] // blocks
    level = (2 * symbols_ref[step, lane : lane + 1, :] - 3).astype(F32) / 3.0
    return cells_ref[0, :, b : b + 1] * level


def core_half(core, x):
    half = x.shape[-1] // 2
    return pick(core, x[..., half:], x[..., :half])


def chip_rows(core, own, other):
    own, other = core_half(core, own), core_half(core, other)
    return jnp.concatenate([pick(core, other, own), pick(core, own, other)], axis=0)


def send_totals(wide_ref, message):
    clusters, ranks, _ = wide_ref.shape
    power = exponent(functools.reduce(jnp.maximum, [top(wide_ref[g]) for g in range(clusters)]))
    for g in range(clusters):
        message[g * ranks : (g + 1) * ranks, :] = encode(wide_ref[g], power)
    put_powers(message.at[clusters * ranks :, :], power, power)


def first_kernel(
    meta, current, voltage, port, resist, elast, symbols, source, target,
    excite_ref, cells_ref, damp_ref, source_ref, target_ref, cur, vol, flat, syms, turned, sems,
):
    blocks, share, _ = current.shape
    col = meta[2]
    pairs = [(port, flat.at[0]), (resist, flat.at[1]), (elast, flat.at[2]), (symbols, syms)]
    pairs += [(current, cur), (voltage, vol), (source, source_ref), (target, target_ref)]
    copies = [pltpu.make_async_copy(*pair, sems.at[k]) for k, pair in enumerate(pairs)]
    for copy in copies:
        copy.start()
    for k in range(3):
        copies[k].wait()
        turned[k] = flat[k].T
        cells_ref[k] = turned[k, pl.ds(pl.multiple_of(meta[1] * 2 * share, 2 * share), 2 * share), :]
    damp_ref[...] = turned[1] + turned[2]
    for copy in copies[3:6]:
        copy.wait()
    here = pl.ds(pl.multiple_of(col * share, share), share)
    port_own, resist_own = turned[0, here, :], turned[1, here, :]
    for b in range(blocks):
        lane = b * symbols.shape[1] // blocks
        level = (2 * syms[0, lane : lane + 1, :] - 3).astype(F32) / 3.0
        excite = port_own[:, b : b + 1] * level - resist_own[:, b : b + 1] * cur[b] - vol[b]
        excite_ref[b] = excite.astype(BF)
    for copy in copies[6:]:
        copy.wait()


def source_kernel(meta, own, other, basis, excite_ref, message, keep_ref, ready):
    blocks, share = own.shape[:2]
    half, rank = excite_ref.shape[2], basis.shape[1] // 2
    core, row = meta[0], meta[1]
    bound = jnp.zeros((8, half), F32)
    for b in range(blocks):
        excite = chip_rows(core, own[b], other[b])
        excite_ref[b] = excite
        side = basis[b, :, pl.ds(pl.multiple_of(row * 2 * share, 2 * share), 2 * share)]
        part = jnp.dot(side, excite, preferred_element_type=F32)
        keep_ref[b] = pick(row, part[rank:], part[:rank])
        sent = pick(row, part[:rank], part[rank:])
        ready[b] = sent
        bound = jnp.maximum(bound, top(sent))
    power = exponent(bound)
    for b in range(blocks):
        message[b * rank : (b + 1) * rank, :] = encode(ready[b], power)
    put_powers(message.at[blocks * rank :, :], power, power)


def layout_kernel(meta, current, current_other, voltage, voltage_other, current_ref, voltage_ref, held, sems):
    sources = (current, current_other, voltage, voltage_other)
    copies = [pltpu.make_async_copy(source, held.at[k], sems.at[k]) for k, source in enumerate(sources)]
    for copy in copies:
        copy.start()
    for copy in copies:
        copy.wait()
    for b in range(current.shape[0]):
        current_ref[b] = chip_rows(meta[0], held[0, b], held[1, b])
        voltage_ref[b] = chip_rows(meta[0], held[2, b], held[3, b])


def stage_kernel(first, second, first_ref, second_ref, sems):
    copies = [
        pltpu.make_async_copy(first, first_ref, sems.at[0]),
        pltpu.make_async_copy(second, second_ref, sems.at[1]),
    ]
    for copy in copies:
        copy.start()
    for copy in copies:
        copy.wait()


def cluster_kernel(member, kept, got, wide_ref, message):
    blocks, ranks, _ = kept.shape
    power, _ = get_powers(got.at[blocks * ranks :, :])
    wide_ref[...] = jnp.zeros(wide_ref.shape, F32)
    for b in range(blocks):
        wide_ref[member[b]] += kept[b] + decode(got[b * ranks : (b + 1) * ranks, :], power)
    send_totals(wide_ref, message)


def add_kernel(wide, got, wide_ref, message):
    clusters, ranks, _ = wide.shape
    power, _ = get_powers(got.at[clusters * ranks :, :])
    for g in range(clusters):
        wide_ref[g] = wide[g] + decode(got[g * ranks : (g + 1) * ranks, :], power)
    send_totals(wide_ref, message)


def translate_kernel(meta, member, wide, got, translation, chosen_ref, totals, rows):
    clusters, ranks, scen = wide.shape
    row = meta[1]
    power, _ = get_powers(got.at[clusters * ranks :, :])
    for g in range(clusters):
        high, low = split(wide[g] + decode(got[g * ranks : (g + 1) * ranks, :], power))
        both = jnp.concatenate([high, low], axis=1)
        none = jnp.zeros(both.shape, BF)
        totals[2 * g * ranks : (2 * g + 1) * ranks, :] = pick(row, none, both)
        totals[(2 * g + 1) * ranks : (2 * g + 2) * ranks, :] = pick(row, both, none)
    blocks, rank = chosen_ref.shape[:2]
    for b in range(blocks):
        rows[b * rank : (b + 1) * rank, :] = translation[
            pl.ds(pl.multiple_of(member[b] * rank, rank), rank), :
        ]
    both = jnp.dot(rows[...], totals[...], preferred_element_type=F32)
    for b in range(blocks):
        block = both[b * rank : (b + 1) * rank]
        chosen_ref[b] = block[:, :scen] + block[:, scen:]


def near_kernel(meta, places, induct, induct_other, own, pair, past, part_ref, around, stacked):
    blocks, rows = own.shape[:2]
    entries, share = places.shape[1], rows // 2
    for k, side in enumerate((meta[0], 1 - meta[0])):
        here = pl.ds(pl.multiple_of(side * share, share), share)
        for n, source in enumerate((own, pair, past)):
            for b in range(blocks):
                around[k, n * blocks + b] = source[b, here, :]
        around[k, 3 * blocks] = jnp.zeros(around.shape[2:], BF)
    for t in range(blocks):
        parts = []
        for k, matrix in enumerate((induct, induct_other)):
            for j in range(entries):
                stacked[t % 2, k, j * share : (j + 1) * share, :] = around[k, places[t, j]]
            parts.append(
                lax.dot_general(
                    stacked[t % 2, k], matrix[t], (((0,), (0,)), ((), ())), preferred_element_type=F32
                )
            )
        part_ref[t] = (parts[0] + parts[1]).T


def finish_kernel(step, last, meta, part, chosen, target, *refs):
    blocks, cells, scen = part.shape
    row = meta[1]
    if last:
        message, keep_ref, ready = refs
    else:
        current, voltage, cells_ref, damp, symbols, basis = refs[:6]
        message, keep_ref, coef_ref, ready, ready_coefs, change = refs[6:]
    rows = cells // 2
    bound = jnp.zeros((8, scen), F32)
    second = jnp.zeros((8, scen), F32)
    for b in range(blocks):
        high, low = split(chosen[b])
        total = part[b] + lax.dot_general(
            jnp.concatenate([target[b], target[b]], axis=0),
            jnp.concatenate([high, low], axis=0),
            (((0,), (0,)), ((), ())),
            preferred_element_type=F32,
        )
        keep_ref[b] = pick(row, total[rows:], total[:rows])
        sent = pick(row, total[:rows], total[rows:])
        ready[b] = sent
        bound = jnp.maximum(bound, top(sent))
        if not last:
            change[b] = -damp[:, b : b + 1] * total
            here = pl.ds(pl.multiple_of(row * rows, rows), rows)
            change[b, here, :] += (
                drive(step + 1, b, blocks, symbols, cells_ref)
                - voltage[b]
                - (cells_ref[1, :, b : b + 1] + cells_ref[2, :, b : b + 1]) * current[b]
            )
    if not last:
        for b in range(blocks):
            high, low = split(change[b])
            coefs = jnp.dot(
                jnp.concatenate([basis[b], basis[b]], axis=1),
                jnp.concatenate([high, low], axis=0),
                preferred_element_type=F32,
            )
            rank = coefs.shape[0] // 2
            coef_ref[b] = pick(row, coefs[rank:], coefs[:rank])
            sent = pick(row, coefs[:rank], coefs[rank:])
            ready_coefs[b] = sent
            second = jnp.maximum(second, top(sent))
    power, second = exponent(bound), exponent(second)
    for b in range(blocks):
        message[b * rows : (b + 1) * rows, :] = encode(ready[b], power)
    if not last:
        start, rank = blocks * rows, ready_coefs.shape[1]
        for b in range(blocks):
            message[start + b * rank : start + (b + 1) * rank, :] = encode(ready_coefs[b], second)
    put_powers(message.at[message.shape[0] - TILE :, :], power, second)


def update_kernel(step, last, *refs):
    if last:
        meta, current, voltage, kept, got, cells, mine_ref, sent_ref = refs
    else:
        member, current, voltage, kept, got, cells, coefs, symbols = refs[:8]
        current_ref, voltage_ref, excite_ref, wide_ref, message = refs[8:]
    blocks, rows, _ = current.shape
    power, second = get_powers(got.at[got.shape[0] - TILE :, :])
    for b in range(blocks):
        cur = current[b] + (kept[b] + decode(got[b * rows : (b + 1) * rows, :], power))
        vol = voltage[b] + cells[2, :, b : b + 1] * cur
        if last:
            for k, value in enumerate((cur, vol)):
                low, high = value[: rows // 2], value[rows // 2 :]
                mine_ref[k, b] = pick(meta[0], high, low)
                sent_ref[k, b] = pick(meta[0], low, high)
        else:
            current_ref[b] = cur
            voltage_ref[b] = vol
            excite = drive(step + 1, b, blocks, symbols, cells) - cells[1, :, b : b + 1] * cur - vol
            excite_ref[b] = excite.astype(BF)
    if not last:
        wide_ref[...] = jnp.zeros(wide_ref.shape, F32)
        start, ranks = blocks * rows, coefs.shape[1]
        for b in range(blocks):
            wide_ref[member[b]] += coefs[b] + decode(got[start + b * ranks : start + (b + 1) * ranks, :], second)
        send_totals(wide_ref, message)


def final_kernel(meta, mine, got, current_ref, voltage_ref):
    for k, result in enumerate((current_ref, voltage_ref)):
        for b in range(mine.shape[1]):
            own, other = mine[k, b], got[k, b]
            result[b] = jnp.concatenate([pick(meta[0], other, own), pick(meta[0], own, other)], axis=1)


def swap(array, axis, distance):
    count = lax.axis_size(axis)
    return lax.ppermute(array, axis, [(i, i ^ distance) for i in range(count)])


def pass_on(array, axis):
    count = lax.axis_size(axis)
    up = [(i, i + 2) for i in range(0, count - 2, 2)]
    down = [(i, i - 2) for i in range(3, count, 2)]
    return lax.ppermute(array, axis, up + down)


def per_device(
    current,
    voltage,
    resistance,
    elastance,
    port_gain,
    symbols,
    neighbours,
    live_counts,
    membership,
    inductance_near,
    source_basis,
    target_basis,
    translation,
):
    blocks, entries = neighbours.shape
    share, cells = inductance_near.shape[2:]
    scen = current.shape[2]
    rank = source_basis.shape[1]
    groups = lax.axis_size("cells")
    rows, half, hrank = 2 * share, scen // 2, rank // 2
    group, col = lax.axis_index("cells"), lax.axis_index("cols")
    core = col & 1
    meta = jnp.stack([core, col >> 1, col]).astype(jnp.int32)
    member = membership[:, 0]
    owner = neighbours // blocks
    slot = jnp.where(owner == group, 0, jnp.where(owner == (group ^ 1), 1, 2))
    live = jnp.arange(entries, dtype=jnp.int32)[None, :] < live_counts[:, None]
    places = jnp.where(live, slot * blocks + neighbours % blocks, 3 * blocks).astype(jnp.int32)
    induct = inductance_near.reshape(blocks, entries * share, cells)
    symbols_half = lax.dynamic_slice_in_dim(symbols, core * half, half, 2)

    state_f32 = shaped((blocks, rows, half), F32)
    state_bf = shaped((blocks, rows, half), BF)
    wide_f32 = shaped((CLUSTERS, hrank, half), F32)
    wide_msg = shaped((CLUSTERS * hrank + TILE, half), I16)
    coef_f32 = shaped((blocks, hrank, half), F32)

    first, columns, damp, source_basis, target_basis = local_call(
        first_kernel,
        (
            meta,
            current,
            voltage,
            port_gain,
            resistance,
            elastance,
            symbols,
            source_basis,
            target_basis,
        ),
        (
            shaped((blocks, share, scen), BF),
            shaped((3, rows, blocks), F32),
            shaped((cells, blocks), F32),
            shaped(source_basis.shape, BF),
            shaped(target_basis.shape, BF),
        ),
        scratch=(
            pltpu.VMEM(current.shape, F32),
            pltpu.VMEM(voltage.shape, F32),
            pltpu.VMEM((3,) + port_gain.shape, F32),
            pltpu.VMEM(symbols.shape, jnp.int32),
            pltpu.VMEM((3, cells, blocks), F32),
            pltpu.SemaphoreType.DMA((8,)),
        ),
        scalars=1,
        left=tuple(range(1, 9)),
    )
    first_other = swap(first, "cols", 1)
    excite, send, kept = local_call(
        source_kernel,
        (meta, first, first_other, source_basis),
        (state_bf, shaped((blocks * hrank + TILE, half), I16), coef_f32),
        scratch=(pltpu.VMEM((blocks, hrank, half), F32),),
        scalars=1,
    )
    for step in range(STEPS):
        last = step == STEPS - 1
        pair = swap(excite, "cells", 1)
        if step == 0:
            got = swap(send, "cols", 2)
            later, _ = lax.optimization_barrier(((current, voltage, induct), send))
            current_other, voltage_other, induct_other = (swap(a, "cols", 1) for a in later)
            wide, send = local_call(cluster_kernel, (member, kept, got), (wide_f32, wide_msg), scalars=1)
        distance = 2
        while distance < groups:
            got = swap(send, "cells", distance)
            if step == 0 and distance == 2:
                got, pair = lax.optimization_barrier((got, pair))
            wide, send = local_call(
                add_kernel,
                (wide, got),
                (wide_f32, wide_msg),
                after=(current,) if step == 0 and distance == 4 else (),
            )
            if distance == 2:
                pair, _ = lax.optimization_barrier((pair, send))
            distance *= 2
            if step > 0 or distance != 4:
                continue
            current, voltage = local_call(
                layout_kernel,
                (meta, current, current_other, voltage, voltage_other),
                (state_f32, state_f32),
                scratch=(pltpu.VMEM((4,) + current.shape, F32), pltpu.SemaphoreType.DMA((4,))),
                scalars=1,
                left=(1, 2, 3, 4),
                after=(send,),
            )
        got = swap(send, "cells", 1)
        if step == 0:
            induct_other, translation = local_call(
                stage_kernel,
                (induct_other, translation),
                (shaped(induct.shape, BF), shaped(translation.shape, BF)),
                scratch=(pltpu.SemaphoreType.DMA((2,)),),
                left=(0, 1),
                after=(send,),
            )
        (chosen,) = local_call(
            translate_kernel,
            (meta, member, wide, got, translation),
            (shaped((blocks, rank, half), F32),),
            scratch=(
                pltpu.VMEM((CLUSTERS * rank, scen), BF),
                pltpu.VMEM((blocks * rank, CLUSTERS * rank), BF),
            ),
            scalars=2,
        )
        past = pass_on(pair, "cells")
        (part,) = local_call(
            near_kernel,
            (meta, places, induct, induct_other, excite, pair, past),
            (shaped((blocks, cells, half), F32),),
            scratch=(
                pltpu.VMEM((2, 3 * blocks + 1, share, half), BF),
                pltpu.VMEM((2, 2, entries * share, half), BF),
            ),
            scalars=2,
        )
        if last:
            send, kept = local_call(
                functools.partial(finish_kernel, step, last),
                (meta, part, chosen, target_basis),
                (shaped((blocks * rows + TILE, half), I16), state_f32),
                scratch=(pltpu.VMEM((blocks, rows, half), F32),),
                scalars=1,
            )
            got = swap(send, "cols", 2)
            mine, send = local_call(
                functools.partial(update_kernel, step, last),
                (meta, current, voltage, kept, got, columns),
                (shaped((2, blocks, share, half), F32),) * 2,
                scalars=1,
            )
        else:
            send, kept, coefs = local_call(
                functools.partial(finish_kernel, step, last),
                (meta, part, chosen, target_basis, current, voltage, columns, damp, symbols_half, source_basis),
                (shaped((blocks * (rows + hrank) + TILE, half), I16), state_f32, coef_f32),
                scratch=(
                    pltpu.VMEM((blocks, rows, half), F32),
                    pltpu.VMEM((blocks, hrank, half), F32),
                    pltpu.VMEM((blocks, cells, half), F32),
                ),
                scalars=1,
            )
            got = swap(send, "cols", 2)
            current, voltage, excite, wide, send = local_call(
                functools.partial(update_kernel, step, last),
                (member, current, voltage, kept, got, columns, coefs, symbols_half),
                (state_f32, state_f32, state_bf, wide_f32, wide_msg),
                scalars=1,
            )
    got = swap(send, "cols", 1)
    return local_call(
        final_kernel, (meta, mine, got), (shaped((blocks, share, scen), F32),) * 2, scalars=1
    )


def solution(mesh):
    placed = (
        P("cells", "cols", None),
        P("cells", "cols", None),
        P("cells", None),
        P("cells", None),
        P("cells", None),
        P(None, "cells", None),
        P("cells", None),
        P("cells"),
        P("cells", None),
        P("cells", None, "cols", None),
        P("cells", None, None),
        P("cells", None, None),
        P(),
    )
    return jax.shard_map(
        per_device,
        mesh=mesh,
        in_specs=placed,
        out_specs=(P("cells", "cols", None), P("cells", "cols", None)),
        check_vma=False,
    )
```

```python
import functools

import jax
import jax.numpy as jnp
from jax import lax
from jax.experimental import pallas as pl
from jax.experimental.pallas import tpu as pltpu
from jax.sharding import PartitionSpec as P

CLUSTERS = 16
STEPS = 3
BF = jnp.bfloat16
F32 = jnp.float32
I16 = jnp.int16
TILE = 16
SMEM = pl.BlockSpec(memory_space=pltpu.SMEM)
VMEM = pl.BlockSpec(memory_space=pltpu.VMEM)
HBM = pl.BlockSpec(memory_space=pltpu.HBM)
ANY = pl.BlockSpec(memory_space=pl.ANY)


def local_call(body, ins, outs, scratch=(), scalars=0, after=(), left=()):
    moved = sum(a.size * a.dtype.itemsize for a in ins) + sum(o.size * o.dtype.itemsize for o in outs)
    specs = [SMEM] * scalars + [VMEM] * (len(ins) - scalars) + [ANY] * len(after)
    ins = list(ins)
    for k in left:
        specs[k] = HBM
        ins[k] = pltpu.with_memory_space_constraint(ins[k], pltpu.HBM)

    def run(*refs):
        body(*refs[: len(ins)], *refs[len(ins) + len(after) :])

    return pl.pallas_call(
        run,
        out_shape=tuple(outs),
        in_specs=specs,
        out_specs=tuple(VMEM for _ in outs),
        scratch_shapes=list(scratch),
        compiler_params=pltpu.CompilerParams(vmem_limit_bytes=16 << 20),
        cost_estimate=pl.CostEstimate(flops=0, bytes_accessed=moved, transcendentals=0),
        name=getattr(body, "func", body).__name__,
    )(*ins, *after)


def shaped(shape, dtype):
    return jax.ShapeDtypeStruct(shape, dtype)


def pick(flag, one, zero):
    return jnp.where(flag == 1, one, zero)


def top(x):
    return jnp.max(jnp.abs(x).reshape(x.shape[0] // 8, 8, x.shape[1]), axis=0)


def exponent(bound):
    return jnp.ceil(jnp.log2(jnp.maximum(bound, 1e-30)))


def scaled(x, factor):
    return (x.reshape(x.shape[0] // 8, 8, x.shape[1]) * factor[None]).reshape(x.shape)


def encode(x, power):
    return jnp.round(scaled(x, jnp.exp2(14.0 - power))).astype(jnp.int32).astype(I16)


def decode(x, power):
    return scaled(x.astype(jnp.int32).astype(F32), jnp.exp2(power - 14.0))


def put_powers(ref, first, second):
    ref[...] = jnp.concatenate([first, second], axis=0).astype(jnp.int32).astype(I16)


def get_powers(ref):
    both = ref[...].astype(jnp.int32).astype(F32)
    return both[:8], both[8:]


def split(x):
    high = x.astype(BF)
    return high, (x - high.astype(F32)).astype(BF)


def drive(step, b, blocks, symbols_ref, cells_ref):
    lane = b * symbols_ref.shape[1] // blocks
    level = (2 * symbols_ref[step, lane : lane + 1, :] - 3).astype(F32) / 3.0
    return cells_ref[0, :, b : b + 1] * level


def core_half(core, x):
    half = x.shape[-1] // 2
    return pick(core, x[..., half:], x[..., :half])


def chip_rows(core, own, other):
    own, other = core_half(core, own), core_half(core, other)
    return jnp.concatenate([pick(core, other, own), pick(core, own, other)], axis=0)


def send_totals(wide_ref, message):
    clusters, ranks, _ = wide_ref.shape
    power = exponent(functools.reduce(jnp.maximum, [top(wide_ref[g]) for g in range(clusters)]))
    for g in range(clusters):
        message[g * ranks : (g + 1) * ranks, :] = encode(wide_ref[g], power)
    put_powers(message.at[clusters * ranks :, :], power, power)


def first_kernel(
    meta, current, voltage, port, resist, elast, symbols, source, target,
    excite_ref, cells_ref, damp_ref, source_ref, target_ref, cur, vol, flat, syms, turned, sems,
):
    blocks, share, _ = current.shape
    col = meta[2]
    pairs = [(port, flat.at[0]), (resist, flat.at[1]), (elast, flat.at[2]), (symbols, syms)]
    pairs += [(current, cur), (voltage, vol), (source, source_ref), (target, target_ref)]
    copies = [pltpu.make_async_copy(*pair, sems.at[k]) for k, pair in enumerate(pairs)]
    for copy in copies:
        copy.start()
    for k in range(3):
        copies[k].wait()
        turned[k] = flat[k].T
        cells_ref[k] = turned[k, pl.ds(pl.multiple_of(meta[1] * 2 * share, 2 * share), 2 * share), :]
    damp_ref[...] = turned[1] + turned[2]
    for copy in copies[3:6]:
        copy.wait()
    here = pl.ds(pl.multiple_of(col * share, share), share)
    port_own, resist_own = turned[0, here, :], turned[1, here, :]
    for b in range(blocks):
        lane = b * symbols.shape[1] // blocks
        level = (2 * syms[0, lane : lane + 1, :] - 3).astype(F32) / 3.0
        excite = port_own[:, b : b + 1] * level - resist_own[:, b : b + 1] * cur[b] - vol[b]
        excite_ref[b] = excite.astype(BF)
    for copy in copies[6:]:
        copy.wait()


def source_kernel(meta, own, other, basis, excite_ref, message, keep_ref, ready):
    blocks, share = own.shape[:2]
    half, rank = excite_ref.shape[2], basis.shape[1] // 2
    core, row = meta[0], meta[1]
    bound = jnp.zeros((8, half), F32)
    for b in range(blocks):
        excite = chip_rows(core, own[b], other[b])
        excite_ref[b] = excite
        side = basis[b, :, pl.ds(pl.multiple_of(row * 2 * share, 2 * share), 2 * share)]
        part = jnp.dot(side, excite, preferred_element_type=F32)
        keep_ref[b] = pick(row, part[rank:], part[:rank])
        sent = pick(row, part[:rank], part[rank:])
        ready[b] = sent
        bound = jnp.maximum(bound, top(sent))
    power = exponent(bound)
    for b in range(blocks):
        message[b * rank : (b + 1) * rank, :] = encode(ready[b], power)
    put_powers(message.at[blocks * rank :, :], power, power)


def layout_kernel(meta, current, current_other, voltage, voltage_other, current_ref, voltage_ref, held, sems):
    sources = (current, current_other, voltage, voltage_other)
    copies = [pltpu.make_async_copy(source, held.at[k], sems.at[k]) for k, source in enumerate(sources)]
    for copy in copies:
        copy.start()
    for copy in copies:
        copy.wait()
    for b in range(current.shape[0]):
        current_ref[b] = chip_rows(meta[0], held[0, b], held[1, b])
        voltage_ref[b] = chip_rows(meta[0], held[2, b], held[3, b])


def stage_kernel(member, induct, translation, induct_ref, rows_ref, sems):
    blocks = member.shape[0]
    rank = rows_ref.shape[0] // blocks
    copies = [pltpu.make_async_copy(induct, induct_ref, sems.at[blocks])]
    for b in range(blocks):
        rows = pl.ds(pl.multiple_of(member[b] * rank, rank), rank)
        copies.append(
            pltpu.make_async_copy(
                translation.at[rows, :], rows_ref.at[b * rank : (b + 1) * rank, :], sems.at[b]
            )
        )
    for copy in copies:
        copy.start()
    for copy in copies:
        copy.wait()


def cluster_kernel(member, kept, got, wide_ref, message):
    blocks, ranks, _ = kept.shape
    power, _ = get_powers(got.at[blocks * ranks :, :])
    wide_ref[...] = jnp.zeros(wide_ref.shape, F32)
    for b in range(blocks):
        wide_ref[member[b]] += kept[b] + decode(got[b * ranks : (b + 1) * ranks, :], power)
    send_totals(wide_ref, message)


def add_kernel(wide, got, wide_ref, message):
    clusters, ranks, _ = wide.shape
    power, _ = get_powers(got.at[clusters * ranks :, :])
    for g in range(clusters):
        wide_ref[g] = wide[g] + decode(got[g * ranks : (g + 1) * ranks, :], power)
    send_totals(wide_ref, message)


def near_kernel(meta, places, induct, induct_other, own, pair, past, part_ref, around, stacked):
    blocks, rows = own.shape[:2]
    entries, share = places.shape[1], rows // 2
    for k, side in enumerate((meta[0], 1 - meta[0])):
        here = pl.ds(pl.multiple_of(side * share, share), share)
        for n, source in enumerate((own, pair, past)):
            for b in range(blocks):
                around[k, n * blocks + b] = source[b, here, :]
        around[k, 3 * blocks] = jnp.zeros(around.shape[2:], BF)
    for t in range(blocks):
        parts = []
        for k, matrix in enumerate((induct, induct_other)):
            for j in range(entries):
                stacked[t % 2, k, j * share : (j + 1) * share, :] = around[k, places[t, j]]
            parts.append(
                lax.dot_general(
                    stacked[t % 2, k], matrix[t], (((0,), (0,)), ((), ())), preferred_element_type=F32
                )
            )
        part_ref[t] = (parts[0] + parts[1]).T


def finish_kernel(step, last, meta, wide, got, translation, part, target, *refs):
    blocks, cells, scen = part.shape
    row = meta[1]
    if last:
        message, keep_ref, totals, ready = refs
    else:
        current, voltage, cells_ref, damp, symbols, basis = refs[:6]
        message, keep_ref, coef_ref, totals, ready, ready_coefs, change = refs[6:]
    clusters, ranks, _ = wide.shape
    power, _ = get_powers(got.at[clusters * ranks :, :])
    for g in range(clusters):
        high, low = split(wide[g] + decode(got[g * ranks : (g + 1) * ranks, :], power))
        both = jnp.concatenate([high, low], axis=1)
        none = jnp.zeros(both.shape, BF)
        totals[2 * g * ranks : (2 * g + 1) * ranks, :] = pick(row, none, both)
        totals[(2 * g + 1) * ranks : (2 * g + 2) * ranks, :] = pick(row, both, none)
    both = jnp.dot(translation[...], totals[...], preferred_element_type=F32)
    chosen = both[:, :scen] + both[:, scen:]
    rows, rank = cells // 2, 2 * ranks
    bound = jnp.zeros((8, scen), F32)
    second = jnp.zeros((8, scen), F32)
    for b in range(blocks):
        high, low = split(chosen[b * rank : (b + 1) * rank])
        total = part[b] + lax.dot_general(
            jnp.concatenate([target[b], target[b]], axis=0),
            jnp.concatenate([high, low], axis=0),
            (((0,), (0,)), ((), ())),
            preferred_element_type=F32,
        )
        keep_ref[b] = pick(row, total[rows:], total[:rows])
        sent = pick(row, total[:rows], total[rows:])
        ready[b] = sent
        bound = jnp.maximum(bound, top(sent))
        if not last:
            change[b] = -damp[:, b : b + 1] * total
            here = pl.ds(pl.multiple_of(row * rows, rows), rows)
            change[b, here, :] += (
                drive(step + 1, b, blocks, symbols, cells_ref)
                - voltage[b]
                - (cells_ref[1, :, b : b + 1] + cells_ref[2, :, b : b + 1]) * current[b]
            )
    if not last:
        for b in range(blocks):
            high, low = split(change[b])
            coefs = jnp.dot(
                jnp.concatenate([basis[b], basis[b]], axis=1),
                jnp.concatenate([high, low], axis=0),
                preferred_element_type=F32,
            )
            coef_ref[b] = pick(row, coefs[ranks:], coefs[:ranks])
            sent = pick(row, coefs[:ranks], coefs[ranks:])
            ready_coefs[b] = sent
            second = jnp.maximum(second, top(sent))
    power, second = exponent(bound), exponent(second)
    for b in range(blocks):
        message[b * rows : (b + 1) * rows, :] = encode(ready[b], power)
    if not last:
        start = blocks * rows
        for b in range(blocks):
            message[start + b * ranks : start + (b + 1) * ranks, :] = encode(ready_coefs[b], second)
    put_powers(message.at[message.shape[0] - TILE :, :], power, second)


def update_kernel(step, last, *refs):
    if last:
        meta, current, voltage, kept, got, cells, mine_ref, sent_ref = refs
    else:
        member, current, voltage, kept, got, cells, coefs, symbols = refs[:8]
        current_ref, voltage_ref, excite_ref, wide_ref, message = refs[8:]
    blocks, rows, _ = current.shape
    power, second = get_powers(got.at[got.shape[0] - TILE :, :])
    for b in range(blocks):
        cur = current[b] + (kept[b] + decode(got[b * rows : (b + 1) * rows, :], power))
        vol = voltage[b] + cells[2, :, b : b + 1] * cur
        if last:
            for k, value in enumerate((cur, vol)):
                low, high = value[: rows // 2], value[rows // 2 :]
                mine_ref[k, b] = pick(meta[0], high, low)
                sent_ref[k, b] = pick(meta[0], low, high)
        else:
            current_ref[b] = cur
            voltage_ref[b] = vol
            excite = drive(step + 1, b, blocks, symbols, cells) - cells[1, :, b : b + 1] * cur - vol
            excite_ref[b] = excite.astype(BF)
    if not last:
        wide_ref[...] = jnp.zeros(wide_ref.shape, F32)
        start, ranks = blocks * rows, coefs.shape[1]
        for b in range(blocks):
            wide_ref[member[b]] += coefs[b] + decode(got[start + b * ranks : start + (b + 1) * ranks, :], second)
        send_totals(wide_ref, message)


def final_kernel(meta, mine, got, current_ref, voltage_ref):
    for k, result in enumerate((current_ref, voltage_ref)):
        for b in range(mine.shape[1]):
            own, other = mine[k, b], got[k, b]
            result[b] = jnp.concatenate([pick(meta[0], other, own), pick(meta[0], own, other)], axis=1)


def swap(array, axis, distance):
    count = lax.axis_size(axis)
    return lax.ppermute(array, axis, [(i, i ^ distance) for i in range(count)])


def pass_on(array, axis):
    count = lax.axis_size(axis)
    up = [(i, i + 2) for i in range(0, count - 2, 2)]
    down = [(i, i - 2) for i in range(3, count, 2)]
    return lax.ppermute(array, axis, up + down)


def per_device(
    current,
    voltage,
    resistance,
    elastance,
    port_gain,
    symbols,
    neighbours,
    live_counts,
    membership,
    inductance_near,
    source_basis,
    target_basis,
    translation,
):
    blocks, entries = neighbours.shape
    share, cells = inductance_near.shape[2:]
    scen = current.shape[2]
    rank = source_basis.shape[1]
    groups = lax.axis_size("cells")
    rows, half, hrank = 2 * share, scen // 2, rank // 2
    group, col = lax.axis_index("cells"), lax.axis_index("cols")
    core = col & 1
    meta = jnp.stack([core, col >> 1, col]).astype(jnp.int32)
    member = jnp.minimum(membership[:, 0], CLUSTERS - 1)
    owner = neighbours // blocks
    slot = jnp.where(owner == group, 0, jnp.where(owner == (group ^ 1), 1, 2))
    live = jnp.arange(entries, dtype=jnp.int32)[None, :] < live_counts[:, None]
    places = jnp.where(live, slot * blocks + neighbours % blocks, 3 * blocks).astype(jnp.int32)
    induct = inductance_near.reshape(blocks, entries * share, cells)
    symbols_half = lax.dynamic_slice_in_dim(symbols, core * half, half, 2)

    state_f32 = shaped((blocks, rows, half), F32)
    state_bf = shaped((blocks, rows, half), BF)
    wide_f32 = shaped((CLUSTERS, hrank, half), F32)
    wide_msg = shaped((CLUSTERS * hrank + TILE, half), I16)
    coef_f32 = shaped((blocks, hrank, half), F32)
    totals = pltpu.VMEM((CLUSTERS * rank, scen), BF)

    first, columns, damp, source_basis, target_basis = local_call(
        first_kernel,
        (
            meta,
            current,
            voltage,
            port_gain,
            resistance,
            elastance,
            symbols,
            source_basis,
            target_basis,
        ),
        (
            shaped((blocks, share, scen), BF),
            shaped((3, rows, blocks), F32),
            shaped((cells, blocks), F32),
            shaped(source_basis.shape, BF),
            shaped(target_basis.shape, BF),
        ),
        scratch=(
            pltpu.VMEM(current.shape, F32),
            pltpu.VMEM(voltage.shape, F32),
            pltpu.VMEM((3,) + port_gain.shape, F32),
            pltpu.VMEM(symbols.shape, jnp.int32),
            pltpu.VMEM((3, cells, blocks), F32),
            pltpu.SemaphoreType.DMA((8,)),
        ),
        scalars=1,
        left=tuple(range(1, 9)),
    )
    first_other = swap(first, "cols", 1)
    excite, send, kept = local_call(
        source_kernel,
        (meta, first, first_other, source_basis),
        (state_bf, shaped((blocks * hrank + TILE, half), I16), coef_f32),
        scratch=(pltpu.VMEM((blocks, hrank, half), F32),),
        scalars=1,
    )
    for step in range(STEPS):
        last = step == STEPS - 1
        if step == 0:
            got = swap(send, "cols", 2)
        pair = swap(excite, "cells", 1)
        if step == 0:
            later, _ = lax.optimization_barrier(((current, voltage, induct), send))
            current_other, voltage_other, induct_other = (swap(a, "cols", 1) for a in later)
            wide, send = local_call(cluster_kernel, (member, kept, got), (wide_f32, wide_msg), scalars=1)
        distance = 2
        while distance < groups:
            got = swap(send, "cells", distance)
            wide, send = local_call(
                add_kernel,
                (wide, got),
                (wide_f32, wide_msg),
                after={4: (current,)}.get(distance, ()) if step == 0 else (),
            )
            if distance == 2:
                pair, _ = lax.optimization_barrier((pair, send))
            distance *= 2
            if step > 0 or distance != 4:
                continue
            current, voltage = local_call(
                layout_kernel,
                (meta, current, current_other, voltage, voltage_other),
                (state_f32, state_f32),
                scratch=(pltpu.VMEM((4,) + current.shape, F32), pltpu.SemaphoreType.DMA((4,))),
                scalars=1,
                left=(1, 2, 3, 4),
                after=(send,),
            )
        far_got = swap(send, "cells", 1)
        if step == 0:
            induct_other, translation = local_call(
                stage_kernel,
                (member, induct_other, translation),
                (shaped(induct.shape, BF), shaped((blocks * rank, translation.shape[1]), BF)),
                scratch=(pltpu.SemaphoreType.DMA((blocks + 1,)),),
                scalars=1,
                left=(1, 2),
                after=(send,),
            )
        past = pass_on(pair, "cells")
        (part,) = local_call(
            near_kernel,
            (meta, places, induct, induct_other, excite, pair, past),
            (shaped((blocks, cells, half), F32),),
            scratch=(
                pltpu.VMEM((2, 3 * blocks + 1, share, half), BF),
                pltpu.VMEM((2, 2, entries * share, half), BF),
            ),
            scalars=2,
        )
        far_got, part = lax.optimization_barrier((far_got, part))
        if last:
            send, kept = local_call(
                functools.partial(finish_kernel, step, last),
                (meta, wide, far_got, translation, part, target_basis),
                (shaped((blocks * rows + TILE, half), I16), state_f32),
                scratch=(totals, pltpu.VMEM((blocks, rows, half), F32)),
                scalars=1,
            )
            got = swap(send, "cols", 2)
            mine, send = local_call(
                functools.partial(update_kernel, step, last),
                (meta, current, voltage, kept, got, columns),
                (shaped((2, blocks, share, half), F32),) * 2,
                scalars=1,
            )
        else:
            send, kept, coefs = local_call(
                functools.partial(finish_kernel, step, last),
                (
                    meta,
                    wide,
                    far_got,
                    translation,
                    part,
                    target_basis,
                    current,
                    voltage,
                    columns,
                    damp,
                    symbols_half,
                    source_basis,
                ),
                (shaped((blocks * (rows + hrank) + TILE, half), I16), state_f32, coef_f32),
                scratch=(
                    totals,
                    pltpu.VMEM((blocks, rows, half), F32),
                    pltpu.VMEM((blocks, hrank, half), F32),
                    pltpu.VMEM((blocks, cells, half), F32),
                ),
                scalars=1,
            )
            got = swap(send, "cols", 2)
            current, voltage, excite, wide, send = local_call(
                functools.partial(update_kernel, step, last),
                (member, current, voltage, kept, got, columns, coefs, symbols_half),
                (state_f32, state_f32, state_bf, wide_f32, wide_msg),
                scalars=1,
            )
    got = swap(send, "cols", 1)
    return local_call(
        final_kernel, (meta, mine, got), (shaped((blocks, share, scen), F32),) * 2, scalars=1
    )


def solution(mesh):
    placed = (
        P("cells", "cols", None),
        P("cells", "cols", None),
        P("cells", None),
        P("cells", None),
        P("cells", None),
        P(None, "cells", None),
        P("cells", None),
        P("cells"),
        P("cells", None),
        P("cells", None, "cols", None),
        P("cells", None, None),
        P("cells", None, None),
        P(),
    )
    return jax.shard_map(
        per_device,
        mesh=mesh,
        in_specs=placed,
        out_specs=(P("cells", "cols", None), P("cells", "cols", None)),
        check_vma=False,
    )
```

```python
import functools

import jax
import jax.numpy as jnp
from jax import lax
from jax.experimental import pallas as pl
from jax.experimental.pallas import tpu as pltpu
from jax.sharding import PartitionSpec as P

CLUSTERS = 16
STEPS = 3
BF = jnp.bfloat16
F32 = jnp.float32
I16 = jnp.int16
TILE = 16
SMEM = pl.BlockSpec(memory_space=pltpu.SMEM)
VMEM = pl.BlockSpec(memory_space=pltpu.VMEM)
HBM = pl.BlockSpec(memory_space=pltpu.HBM)
ANY = pl.BlockSpec(memory_space=pl.ANY)


def local_call(body, ins, outs, scratch=(), scalars=0, after=(), left=()):
    moved = sum(a.size * a.dtype.itemsize for a in ins) + sum(o.size * o.dtype.itemsize for o in outs)
    specs = [SMEM] * scalars + [VMEM] * (len(ins) - scalars) + [ANY] * len(after)
    ins = list(ins)
    for k in left:
        specs[k] = HBM
        ins[k] = pltpu.with_memory_space_constraint(ins[k], pltpu.HBM)

    def run(*refs):
        body(*refs[: len(ins)], *refs[len(ins) + len(after) :])

    return pl.pallas_call(
        run,
        out_shape=tuple(outs),
        in_specs=specs,
        out_specs=tuple(VMEM for _ in outs),
        scratch_shapes=list(scratch),
        compiler_params=pltpu.CompilerParams(vmem_limit_bytes=16 << 20),
        cost_estimate=pl.CostEstimate(flops=0, bytes_accessed=moved, transcendentals=0),
        name=getattr(body, "func", body).__name__,
    )(*ins, *after)


def shaped(shape, dtype):
    return jax.ShapeDtypeStruct(shape, dtype)


def pick(flag, one, zero):
    return jnp.where(flag == 1, one, zero)


def top(x):
    return jnp.max(jnp.abs(x).reshape(x.shape[0] // 8, 8, x.shape[1]), axis=0)


def exponent(bound):
    return jnp.ceil(jnp.log2(jnp.maximum(bound, 1e-30)))


def scaled(x, factor):
    return (x.reshape(x.shape[0] // 8, 8, x.shape[1]) * factor[None]).reshape(x.shape)


def encode(x, power):
    return jnp.round(scaled(x, jnp.exp2(14.0 - power))).astype(jnp.int32).astype(I16)


def decode(x, power):
    return scaled(x.astype(jnp.int32).astype(F32), jnp.exp2(power - 14.0))


def put_powers(ref, first, second):
    ref[...] = jnp.concatenate([first, second], axis=0).astype(jnp.int32).astype(I16)


def get_powers(ref):
    both = ref[...].astype(jnp.int32).astype(F32)
    return both[:8], both[8:]


def split(x):
    high = x.astype(BF)
    return high, (x - high.astype(F32)).astype(BF)


def drive(step, b, blocks, symbols_ref, cells_ref):
    lane = b * symbols_ref.shape[1] // blocks
    level = (2 * symbols_ref[step, lane : lane + 1, :] - 3).astype(F32) / 3.0
    return cells_ref[0, :, b : b + 1] * level


def core_half(core, x):
    half = x.shape[-1] // 2
    return pick(core, x[..., half:], x[..., :half])


def chip_rows(core, own, other):
    own, other = core_half(core, own), core_half(core, other)
    return jnp.concatenate([pick(core, other, own), pick(core, own, other)], axis=0)


def send_totals(wide_ref, message):
    clusters, ranks, _ = wide_ref.shape
    power = exponent(functools.reduce(jnp.maximum, [top(wide_ref[g]) for g in range(clusters)]))
    for g in range(clusters):
        message[g * ranks : (g + 1) * ranks, :] = encode(wide_ref[g], power)
    put_powers(message.at[clusters * ranks :, :], power, power)


def first_kernel(
    meta, current, voltage, port, resist, elast, symbols, source, target,
    excite_ref, cells_ref, damp_ref, source_ref, target_ref, cur, vol, flat, syms, turned, sems,
):
    blocks, share, _ = current.shape
    col = meta[2]
    pairs = [(port, flat.at[0]), (resist, flat.at[1]), (elast, flat.at[2]), (symbols, syms)]
    pairs += [(current, cur), (voltage, vol), (source, source_ref), (target, target_ref)]
    copies = [pltpu.make_async_copy(*pair, sems.at[k]) for k, pair in enumerate(pairs)]
    for copy in copies:
        copy.start()
    for k in range(3):
        copies[k].wait()
        turned[k] = flat[k].T
        cells_ref[k] = turned[k, pl.ds(pl.multiple_of(meta[1] * 2 * share, 2 * share), 2 * share), :]
    damp_ref[...] = turned[1] + turned[2]
    for copy in copies[3:6]:
        copy.wait()
    here = pl.ds(pl.multiple_of(col * share, share), share)
    port_own, resist_own = turned[0, here, :], turned[1, here, :]
    for b in range(blocks):
        lane = b * symbols.shape[1] // blocks
        level = (2 * syms[0, lane : lane + 1, :] - 3).astype(F32) / 3.0
        excite = port_own[:, b : b + 1] * level - resist_own[:, b : b + 1] * cur[b] - vol[b]
        excite_ref[b] = excite.astype(BF)
    for copy in copies[6:]:
        copy.wait()


def source_kernel(meta, own, other, basis, excite_ref, message, keep_ref, ready):
    blocks, share = own.shape[:2]
    half, rank = excite_ref.shape[2], basis.shape[1] // 2
    core, row = meta[0], meta[1]
    bound = jnp.zeros((8, half), F32)
    for b in range(blocks):
        excite = chip_rows(core, own[b], other[b])
        excite_ref[b] = excite
        side = basis[b, :, pl.ds(pl.multiple_of(row * 2 * share, 2 * share), 2 * share)]
        part = jnp.dot(side, excite, preferred_element_type=F32)
        keep_ref[b] = pick(row, part[rank:], part[:rank])
        sent = pick(row, part[:rank], part[rank:])
        ready[b] = sent
        bound = jnp.maximum(bound, top(sent))
    power = exponent(bound)
    for b in range(blocks):
        message[b * rank : (b + 1) * rank, :] = encode(ready[b], power)
    put_powers(message.at[blocks * rank :, :], power, power)


def layout_kernel(meta, current, current_other, voltage, voltage_other, current_ref, voltage_ref, held, sems):
    sources = (current, current_other, voltage, voltage_other)
    copies = [pltpu.make_async_copy(source, held.at[k], sems.at[k]) for k, source in enumerate(sources)]
    for copy in copies:
        copy.start()
    for copy in copies:
        copy.wait()
    for b in range(current.shape[0]):
        current_ref[b] = chip_rows(meta[0], held[0, b], held[1, b])
        voltage_ref[b] = chip_rows(meta[0], held[2, b], held[3, b])


def stage_kernel(member, induct, translation, induct_ref, rows_ref, sems):
    blocks = member.shape[0]
    rank = rows_ref.shape[0] // blocks
    copies = [pltpu.make_async_copy(induct, induct_ref, sems.at[blocks])]
    for b in range(blocks):
        rows = pl.ds(pl.multiple_of(member[b] * rank, rank), rank)
        copies.append(
            pltpu.make_async_copy(
                translation.at[rows, :], rows_ref.at[b * rank : (b + 1) * rank, :], sems.at[b]
            )
        )
    for copy in copies:
        copy.start()
    for copy in copies:
        copy.wait()


def cluster_kernel(member, kept, got, wide_ref, message):
    blocks, ranks, _ = kept.shape
    power, _ = get_powers(got.at[blocks * ranks :, :])
    wide_ref[...] = jnp.zeros(wide_ref.shape, F32)
    for b in range(blocks):
        wide_ref[member[b]] += kept[b] + decode(got[b * ranks : (b + 1) * ranks, :], power)
    send_totals(wide_ref, message)


def add_kernel(wide, got, wide_ref, message):
    clusters, ranks, _ = wide.shape
    power, _ = get_powers(got.at[clusters * ranks :, :])
    for g in range(clusters):
        wide_ref[g] = wide[g] + decode(got[g * ranks : (g + 1) * ranks, :], power)
    send_totals(wide_ref, message)


def near_kernel(meta, places, induct, induct_other, own, pair, past, part_ref, around, stacked):
    blocks, rows = own.shape[:2]
    entries, share = places.shape[1], rows // 2
    for k, side in enumerate((meta[0], 1 - meta[0])):
        here = pl.ds(pl.multiple_of(side * share, share), share)
        for n, source in enumerate((own, pair, past)):
            for b in range(blocks):
                around[k, n * blocks + b] = source[b, here, :]
        around[k, 3 * blocks] = jnp.zeros(around.shape[2:], BF)
    for t in range(blocks):
        parts = []
        for k, matrix in enumerate((induct, induct_other)):
            for j in range(entries):
                stacked[t % 2, k, j * share : (j + 1) * share, :] = around[k, places[t, j]]
            parts.append(
                lax.dot_general(
                    stacked[t % 2, k], matrix[t], (((0,), (0,)), ((), ())), preferred_element_type=F32
                )
            )
        part_ref[t] = (parts[0] + parts[1]).T


def finish_kernel(step, last, meta, wide, got, translation, part, target, *refs):
    blocks, cells, scen = part.shape
    row = meta[1]
    if last:
        message, keep_ref, totals, ready = refs
    else:
        current, voltage, cells_ref, damp, symbols, basis = refs[:6]
        message, keep_ref, coef_ref, totals, ready, ready_coefs, change = refs[6:]
    clusters, ranks, _ = wide.shape
    power, _ = get_powers(got.at[clusters * ranks :, :])
    for g in range(clusters):
        high, low = split(wide[g] + decode(got[g * ranks : (g + 1) * ranks, :], power))
        both = jnp.concatenate([high, low], axis=1)
        none = jnp.zeros(both.shape, BF)
        totals[2 * g * ranks : (2 * g + 1) * ranks, :] = pick(row, none, both)
        totals[(2 * g + 1) * ranks : (2 * g + 2) * ranks, :] = pick(row, both, none)
    both = jnp.dot(translation[...], totals[...], preferred_element_type=F32)
    chosen = both[:, :scen] + both[:, scen:]
    rows, rank = cells // 2, 2 * ranks
    bound = jnp.zeros((8, scen), F32)
    second = jnp.zeros((8, scen), F32)
    for b in range(blocks):
        high, low = split(chosen[b * rank : (b + 1) * rank])
        total = part[b] + lax.dot_general(
            jnp.concatenate([target[b], target[b]], axis=0),
            jnp.concatenate([high, low], axis=0),
            (((0,), (0,)), ((), ())),
            preferred_element_type=F32,
        )
        keep_ref[b] = pick(row, total[rows:], total[:rows])
        sent = pick(row, total[:rows], total[rows:])
        ready[b] = sent
        bound = jnp.maximum(bound, top(sent))
        if not last:
            change[b] = -damp[:, b : b + 1] * total
            here = pl.ds(pl.multiple_of(row * rows, rows), rows)
            change[b, here, :] += (
                drive(step + 1, b, blocks, symbols, cells_ref)
                - voltage[b]
                - (cells_ref[1, :, b : b + 1] + cells_ref[2, :, b : b + 1]) * current[b]
            )
    if not last:
        for b in range(blocks):
            coefs = jnp.dot(basis[b], change[b].astype(BF), preferred_element_type=F32)
            coef_ref[b] = pick(row, coefs[ranks:], coefs[:ranks])
            sent = pick(row, coefs[:ranks], coefs[ranks:])
            ready_coefs[b] = sent
            second = jnp.maximum(second, top(sent))
    power, second = exponent(bound), exponent(second)
    for b in range(blocks):
        message[b * rows : (b + 1) * rows, :] = encode(ready[b], power)
    if not last:
        start = blocks * rows
        for b in range(blocks):
            message[start + b * ranks : start + (b + 1) * ranks, :] = encode(ready_coefs[b], second)
    put_powers(message.at[message.shape[0] - TILE :, :], power, second)


def update_kernel(step, last, *refs):
    if last:
        meta, current, voltage, kept, got, cells, mine_ref, sent_ref = refs
    else:
        member, current, voltage, kept, got, cells, coefs, symbols = refs[:8]
        current_ref, voltage_ref, excite_ref, wide_ref, message = refs[8:]
    blocks, rows, _ = current.shape
    power, second = get_powers(got.at[got.shape[0] - TILE :, :])
    for b in range(blocks):
        cur = current[b] + (kept[b] + decode(got[b * rows : (b + 1) * rows, :], power))
        vol = voltage[b] + cells[2, :, b : b + 1] * cur
        if last:
            for k, value in enumerate((cur, vol)):
                low, high = value[: rows // 2], value[rows // 2 :]
                mine_ref[k, b] = pick(meta[0], high, low)
                sent_ref[k, b] = pick(meta[0], low, high)
        else:
            current_ref[b] = cur
            voltage_ref[b] = vol
            excite = drive(step + 1, b, blocks, symbols, cells) - cells[1, :, b : b + 1] * cur - vol
            excite_ref[b] = excite.astype(BF)
    if not last:
        wide_ref[...] = jnp.zeros(wide_ref.shape, F32)
        start, ranks = blocks * rows, coefs.shape[1]
        for b in range(blocks):
            wide_ref[member[b]] += coefs[b] + decode(got[start + b * ranks : start + (b + 1) * ranks, :], second)
        send_totals(wide_ref, message)


def final_kernel(meta, mine, got, current_ref, voltage_ref):
    for k, result in enumerate((current_ref, voltage_ref)):
        for b in range(mine.shape[1]):
            own, other = mine[k, b], got[k, b]
            result[b] = jnp.concatenate([pick(meta[0], other, own), pick(meta[0], own, other)], axis=1)


def swap(array, axis, distance):
    count = lax.axis_size(axis)
    return lax.ppermute(array, axis, [(i, i ^ distance) for i in range(count)])


def pass_on(array, axis):
    count = lax.axis_size(axis)
    up = [(i, i + 2) for i in range(0, count - 2, 2)]
    down = [(i, i - 2) for i in range(3, count, 2)]
    return lax.ppermute(array, axis, up + down)


def per_device(
    current,
    voltage,
    resistance,
    elastance,
    port_gain,
    symbols,
    neighbours,
    live_counts,
    membership,
    inductance_near,
    source_basis,
    target_basis,
    translation,
):
    blocks, entries = neighbours.shape
    share, cells = inductance_near.shape[2:]
    scen = current.shape[2]
    rank = source_basis.shape[1]
    groups = lax.axis_size("cells")
    rows, half, hrank = 2 * share, scen // 2, rank // 2
    group, col = lax.axis_index("cells"), lax.axis_index("cols")
    core = col & 1
    meta = jnp.stack([core, col >> 1, col]).astype(jnp.int32)
    member = jnp.minimum(membership[:, 0], CLUSTERS - 1)
    owner = neighbours // blocks
    slot = jnp.where(owner == group, 0, jnp.where(owner == (group ^ 1), 1, 2))
    live = jnp.arange(entries, dtype=jnp.int32)[None, :] < live_counts[:, None]
    places = jnp.where(live, slot * blocks + neighbours % blocks, 3 * blocks).astype(jnp.int32)
    induct = inductance_near.reshape(blocks, entries * share, cells)
    symbols_half = lax.dynamic_slice_in_dim(symbols, core * half, half, 2)

    state_f32 = shaped((blocks, rows, half), F32)
    state_bf = shaped((blocks, rows, half), BF)
    wide_f32 = shaped((CLUSTERS, hrank, half), F32)
    wide_msg = shaped((CLUSTERS * hrank + TILE, half), I16)
    coef_f32 = shaped((blocks, hrank, half), F32)
    totals = pltpu.VMEM((CLUSTERS * rank, scen), BF)

    first, columns, damp, source_basis, target_basis = local_call(
        first_kernel,
        (
            meta,
            current,
            voltage,
            port_gain,
            resistance,
            elastance,
            symbols,
            source_basis,
            target_basis,
        ),
        (
            shaped((blocks, share, scen), BF),
            shaped((3, rows, blocks), F32),
            shaped((cells, blocks), F32),
            shaped(source_basis.shape, BF),
            shaped(target_basis.shape, BF),
        ),
        scratch=(
            pltpu.VMEM(current.shape, F32),
            pltpu.VMEM(voltage.shape, F32),
            pltpu.VMEM((3,) + port_gain.shape, F32),
            pltpu.VMEM(symbols.shape, jnp.int32),
            pltpu.VMEM((3, cells, blocks), F32),
            pltpu.SemaphoreType.DMA((8,)),
        ),
        scalars=1,
        left=tuple(range(1, 9)),
    )
    first_other = swap(first, "cols", 1)
    excite, send, kept = local_call(
        source_kernel,
        (meta, first, first_other, source_basis),
        (state_bf, shaped((blocks * hrank + TILE, half), I16), coef_f32),
        scratch=(pltpu.VMEM((blocks, hrank, half), F32),),
        scalars=1,
    )
    for step in range(STEPS):
        last = step == STEPS - 1
        if step == 0:
            got = swap(send, "cols", 2)
        pair = swap(excite, "cells", 1)
        if step == 0:
            later, _ = lax.optimization_barrier(((current, voltage, induct), send))
            current_other, voltage_other, induct_other = (swap(a, "cols", 1) for a in later)
            wide, send = local_call(cluster_kernel, (member, kept, got), (wide_f32, wide_msg), scalars=1)
        distance = 2
        while distance < groups:
            got = swap(send, "cells", distance)
            wide, send = local_call(
                add_kernel,
                (wide, got),
                (wide_f32, wide_msg),
                after={4: (current,)}.get(distance, ()) if step == 0 else (),
            )
            if distance == 2:
                pair, _ = lax.optimization_barrier((pair, send))
            distance *= 2
            if step > 0 or distance != 4:
                continue
            current, voltage = local_call(
                layout_kernel,
                (meta, current, current_other, voltage, voltage_other),
                (state_f32, state_f32),
                scratch=(pltpu.VMEM((4,) + current.shape, F32), pltpu.SemaphoreType.DMA((4,))),
                scalars=1,
                left=(1, 2, 3, 4),
                after=(send,),
            )
        far_got = swap(send, "cells", 1)
        if step == 0:
            induct_other, translation = local_call(
                stage_kernel,
                (member, induct_other, translation),
                (shaped(induct.shape, BF), shaped((blocks * rank, translation.shape[1]), BF)),
                scratch=(pltpu.SemaphoreType.DMA((blocks + 1,)),),
                scalars=1,
                left=(1, 2),
                after=(send,),
            )
        past = pass_on(pair, "cells")
        (part,) = local_call(
            near_kernel,
            (meta, places, induct, induct_other, excite, pair, past),
            (shaped((blocks, cells, half), F32),),
            scratch=(
                pltpu.VMEM((2, 3 * blocks + 1, share, half), BF),
                pltpu.VMEM((2, 2, entries * share, half), BF),
            ),
            scalars=2,
        )
        far_got, part = lax.optimization_barrier((far_got, part))
        if last:
            send, kept = local_call(
                functools.partial(finish_kernel, step, last),
                (meta, wide, far_got, translation, part, target_basis),
                (shaped((blocks * rows + TILE, half), I16), state_f32),
                scratch=(totals, pltpu.VMEM((blocks, rows, half), F32)),
                scalars=1,
            )
            got = swap(send, "cols", 2)
            mine, send = local_call(
                functools.partial(update_kernel, step, last),
                (meta, current, voltage, kept, got, columns),
                (shaped((2, blocks, share, half), F32),) * 2,
                scalars=1,
            )
        else:
            send, kept, coefs = local_call(
                functools.partial(finish_kernel, step, last),
                (
                    meta,
                    wide,
                    far_got,
                    translation,
                    part,
                    target_basis,
                    current,
                    voltage,
                    columns,
                    damp,
                    symbols_half,
                    source_basis,
                ),
                (shaped((blocks * (rows + hrank) + TILE, half), I16), state_f32, coef_f32),
                scratch=(
                    totals,
                    pltpu.VMEM((blocks, rows, half), F32),
                    pltpu.VMEM((blocks, hrank, half), F32),
                    pltpu.VMEM((blocks, cells, half), F32),
                ),
                scalars=1,
            )
            got = swap(send, "cols", 2)
            current, voltage, excite, wide, send = local_call(
                functools.partial(update_kernel, step, last),
                (member, current, voltage, kept, got, columns, coefs, symbols_half),
                (state_f32, state_f32, state_bf, wide_f32, wide_msg),
                scalars=1,
            )
    got = swap(send, "cols", 1)
    return local_call(
        final_kernel, (meta, mine, got), (shaped((blocks, share, scen), F32),) * 2, scalars=1
    )


def solution(mesh):
    placed = (
        P("cells", "cols", None),
        P("cells", "cols", None),
        P("cells", None),
        P("cells", None),
        P("cells", None),
        P(None, "cells", None),
        P("cells", None),
        P("cells"),
        P("cells", None),
        P("cells", None, "cols", None),
        P("cells", None, None),
        P("cells", None, None),
        P(),
    )
    return jax.shard_map(
        per_device,
        mesh=mesh,
        in_specs=placed,
        out_specs=(P("cells", "cols", None), P("cells", "cols", None)),
        check_vma=False,
    )
```
